512 devices in a mesh: blk: 512 (over x, z, y, core).
Axes of the slice: x: 4, y: 8, z: 8, core: 2. Of those that a mesh axis runs over, the one named last changes fastest.
Arguments:
- users: float32 [524288, 128], P('blk'), may hold values from -4 to 4
- user_bias: float32 [524288], P('blk'), may hold values from -6 to 6
- items: float32 [262144, 128], P('blk'), may hold values from -4 to 4
- item_bias: float32 [262144], P('blk'), may hold values from -6 to 6
- global_mean: float32 [], replicated, may hold values from 2 to 4
- item_owner: int32 [2, 512], P(None, 'blk'), may hold values from 0 to 511, as said below
- tile_rows: int32 [2, 512, 16], P(None, 'blk'), may hold values from 0 to 7
- tile_cols: int32 [2, 512, 16], P(None, 'blk'), may hold values from 0 to 3
- tile_counts: int32 [2, 512], P(None, 'blk'), may hold values from 1 to 16, as said below
- ratings: bfloat16 [2, 512, 16, 128, 128], P(None, 'blk'), may hold values from 1 to 5
- observed: int32 [2, 512, 16, 128, 128], P(None, 'blk'), may hold values 0 or 1
Outputs:
- users_out: float32 [524288, 128], P('blk')
- user_bias_out: float32 [524288], P('blk')
- items_out: float32 [262144, 128], P('blk')
- item_bias_out: float32 [262144], P('blk')
- mean_out: float32 [], replicated
The draws below stay inside these ranges and needn't reach their ends.
Inputs may be any that keep to these rules, and one draw needn't show every extreme that they name: For each s there is a number m_s with item_owner[s, b] = b XOR m_s for every b; every bit of a block index is set in some m_s. `tile_counts`: in each sub-epoch some block pair uses all 16 slots.
All inputs are finite; a program needn't handle non-finite values. No bound on the sum of `observed` on one device may be relied on, other than what follows from the above.
Results may differ from the reference program's by a relative error of at most 0.0018.
Values sent between devices are 32-bit elements; how exact they have to be, the bound alone decides.
A program may use at most 64 MiB of HBM per device.

```python
import jax
import jax.numpy as jnp
from jax import lax

R = 128
TILE = 128
U_DEV = 1024
I_DEV = 512
TMAX = 16
SUBEP = 2
USERS = 524288
ITEMS = 262144
N_BLK = 512


def draw_item_owner(key, part):
    key = jax.random.fold_in(key, 11)
    first_key, extra_key, more_key = jax.random.split(key, 3)
    top = N_BLK - 1
    first = jax.random.randint(first_key, (), 0, N_BLK)
    extra = jax.random.randint(extra_key, (), 0, N_BLK)
    masks = jax.random.randint(more_key, (SUBEP,), 0, N_BLK)
    masks = masks.at[0].set(first)
    last = jnp.bitwise_or(jnp.bitwise_and(jnp.bitwise_not(first), top), extra)
    masks = masks.at[SUBEP - 1].set(last)
    blocks = jnp.arange(N_BLK, dtype=jnp.int32)
    return jnp.bitwise_xor(blocks[None, :], masks[:, None]).astype(jnp.int32)


def draw_tile_counts(key, part):
    key = jax.random.fold_in(key, 12)
    count_key, spot_key = jax.random.split(key)
    counts = jax.random.randint(count_key, (SUBEP, N_BLK), 1, TMAX + 1)
    spots = jax.random.randint(spot_key, (SUBEP,), 0, N_BLK)
    counts = counts.at[jnp.arange(SUBEP), spots].set(TMAX)
    return counts.astype(jnp.int32)


def place_ends(values, stream_key, low, high):
    place = [jax.random.randint(jax.random.fold_in(stream_key, axis), (), 0, length) for axis, length in enumerate(values.shape)]
    main_axis = values.shape.index(max(values.shape))
    neighbour = place[:main_axis] + [(place[main_axis] + 1) % values.shape[main_axis]] + place[main_axis + 1:]
    return values.at[tuple(place)].set(low).at[tuple(neighbour)].set(high)


def steps_of(key, shape, cuts, low, top_value):
    gain, own = 1.0, jax.random.fold_in(key, 6)
    for axis_at, parts in cuts:
        heights = jnp.exp(jax.random.uniform(jax.random.fold_in(own, axis_at), (parts,), jnp.float32, low / len(cuts), top_value / len(cuts)))
        gain = gain * jnp.repeat(heights, shape[axis_at] // parts).reshape([-1 if axis == axis_at else 1 for axis in range(len(shape))])
    return gain


def normal_values(key, dims, deviation, limit, cuts=(), kind=jnp.bfloat16):
    loudness = steps_of(key, dims, cuts, -0.22, 0.18) if cuts else 1.0
    array = jax.random.normal(key, dims, jnp.float32) * deviation * loudness
    return jnp.minimum(jnp.maximum(array, -limit), limit).astype(kind)


def setup_inputs(seed: int = 0) -> dict:
    splits = jax.random.split(jax.random.key(seed), 12)
    return {
        "users": normal_values(splits[0], (USERS, R), 0.3, 4.0, ((0, 512),), jnp.float32),
        "user_bias": normal_values(splits[1], (USERS,), 0.5, 6.0, ((0, 512),), jnp.float32),
        "items": normal_values(splits[2], (ITEMS, R), 0.3, 4.0, ((0, 512),), jnp.float32),
        "item_bias": normal_values(splits[3], (ITEMS,), 0.5, 6.0, ((0, 512),), jnp.float32),
        "global_mean": jnp.clip(jax.random.uniform(splits[4], (), jnp.float32, 2.0, 4.0), 2.0, 4.0),
        "item_owner": draw_item_owner(jax.random.fold_in(splits[11], 71), 0),
        "tile_rows": place_ends(jax.random.randint(splits[6], (SUBEP, N_BLK, TMAX), 0, U_DEV // TILE), jax.random.fold_in(splits[6], 1), 0, (U_DEV // TILE) - 1).astype(jnp.int32),
        "tile_cols": place_ends(jax.random.randint(splits[7], (SUBEP, N_BLK, TMAX), 0, I_DEV // TILE), jax.random.fold_in(splits[7], 1), 0, (I_DEV // TILE) - 1).astype(jnp.int32),
        "tile_counts": draw_tile_counts(jax.random.fold_in(splits[11], 71), 0),
        "ratings": jnp.clip(1.0 + 4.0 * jax.random.uniform(splits[9], (SUBEP, N_BLK, TMAX, TILE, TILE), jnp.float32) ** steps_of(splits[9], (SUBEP, N_BLK, TMAX, TILE, TILE), ((1, 512),), -0.2, 0.2), 1.0, 5.0).astype(jnp.bfloat16),
        "observed": place_ends((jax.random.randint(splits[10], (SUBEP, N_BLK, TMAX, TILE, TILE), 0, 2) < 1).astype(jnp.int32), jax.random.fold_in(splits[10], 1), 0, 1),
    }


step_scale = 0.8
bias_rate = 0.005
shrink = 0.02
mean_rate = 0.5


def run_block(users, ubias, items, ibias, mean, rows, cols, count, ratings, observed):
    edge = ratings.shape[-1]
    rank = users.shape[1]
    learn_rate = step_scale / edge

    def step(carry, t):
        users, ubias, items, ibias, err_sum, obs_sum = carry
        row0 = (rows[t] * edge).astype(jnp.int32)
        col0 = (cols[t] * edge).astype(jnp.int32)
        zero = jnp.int32(0)
        u = lax.dynamic_slice(users, (row0, zero), (edge, rank))
        v = lax.dynamic_slice(items, (col0, zero), (edge, rank))
        bu = lax.dynamic_slice_in_dim(ubias, row0, edge)
        bv = lax.dynamic_slice_in_dim(ibias, col0, edge)
        uh = u.astype(jnp.bfloat16)
        vh = v.astype(jnp.bfloat16)
        score = lax.dot_general(uh, vh, (((1,), (1,)), ((), ())), preferred_element_type=jnp.float32)
        obs = observed[t].astype(jnp.float32)
        err = obs * (ratings[t].astype(jnp.float32) - (mean + bu[:, None] + bv[None, :] + score))
        eh = err.astype(jnp.bfloat16)
        grad_u = jnp.dot(eh, vh, preferred_element_type=jnp.float32)
        grad_v = lax.dot_general(eh, uh, (((0,), (0,)), ((), ())), preferred_element_type=jnp.float32)
        active = t < count
        new_u = jnp.where(active, u + learn_rate * (grad_u - shrink * u), u)
        new_v = jnp.where(active, v + learn_rate * (grad_v - shrink * v), v)
        new_bu = jnp.where(active, bu + bias_rate * (jnp.sum(err, axis=1) - shrink * bu), bu)
        new_bv = jnp.where(active, bv + bias_rate * (jnp.sum(err, axis=0) - shrink * bv), bv)
        users = lax.dynamic_update_slice(users, new_u, (row0, zero))
        items = lax.dynamic_update_slice(items, new_v, (col0, zero))
        ubias = lax.dynamic_update_slice_in_dim(ubias, new_bu, row0, 0)
        ibias = lax.dynamic_update_slice_in_dim(ibias, new_bv, col0, 0)
        err_sum = err_sum + jnp.where(active, jnp.sum(err), jnp.float32(0.0))
        obs_sum = obs_sum + jnp.where(active, jnp.sum(obs), jnp.float32(0.0))
        return (users, ubias, items, ibias, err_sum, obs_sum), None

    init = (users, ubias, items, ibias, jnp.float32(0.0), jnp.float32(0.0))
    out, _ = lax.scan(step, init, jnp.arange(rows.shape[0], dtype=jnp.int32))
    return out


def reference(users, user_bias, items, item_bias, global_mean, item_owner, tile_rows, tile_cols, tile_counts, ratings, observed):
    rank = users.shape[1]
    user_blocks = users.reshape(N_BLK, U_DEV, rank)
    ubias_blocks = user_bias.reshape(N_BLK, U_DEV)
    item_blocks = items.reshape(N_BLK, I_DEV, rank)
    ibias_blocks = item_bias.reshape(N_BLK, I_DEV)
    mean = global_mean.astype(jnp.float32)
    for sub in range(SUBEP):
        owner = item_owner[sub]
        paired = item_blocks[owner]
        paired_bias = ibias_blocks[owner]
        result = jax.vmap(run_block, in_axes=(0, 0, 0, 0, None, 0, 0, 0, 0, 0))(
            user_blocks, ubias_blocks, paired, paired_bias, mean,
            tile_rows[sub], tile_cols[sub], tile_counts[sub], ratings[sub], observed[sub])
        user_blocks, ubias_blocks, new_items, new_ibias, err_sums, obs_sums = result
        item_blocks = item_blocks.at[owner].set(new_items)
        ibias_blocks = ibias_blocks.at[owner].set(new_ibias)
        mean = mean + mean_rate * jnp.sum(err_sums) / jnp.sum(obs_sums)
    return (user_blocks.reshape(USERS, rank), ubias_blocks.reshape(USERS),
            item_blocks.reshape(ITEMS, rank), ibias_blocks.reshape(ITEMS), mean)
```

```python
import functools

import jax
import jax.numpy as jnp
from jax import lax
from jax.experimental import pallas as pl
from jax.experimental.pallas import tpu as pltpu
from jax.sharding import PartitionSpec as P

SUBEP = 2
TILE = 128
ROW_TILES = 8
COL_TILES = 4
ITEM_ROWS = COL_TILES * TILE
PACKED = ITEM_ROWS + 8

step_scale = 0.8
bias_rate = 0.005
shrink = 0.02
mean_rate = 0.5

F32 = jnp.float32
BF16 = jnp.bfloat16
MESH = pl.DeviceIdType.MESH

STAGE_A = (1, 2, 3, 7)
STAGE_B = (4, 5, 6, 8)
CORE_BIT = 0
SUM_A = ((1, 2), (2, 8))
SUM_B = ((16, 8), (128, 4))


def flipped(me, bits):
    other = me
    for bit in bits:
        taken = lax.rem(lax.div(me, 1 << bit), 2)
        other = other + (1 - 2 * taken) * (1 << bit)
    return other


def group_peer(me, stride, size, ahead):
    place = lax.rem(lax.div(me, stride), size)
    return me + (lax.rem(place + ahead, size) - place) * stride


def stage_kernel(bits, rounds, x_ref, s_ref, y_ref, t_ref, *scratch):
    held, got = scratch[0], scratch[1 : 1 + len(rounds)]
    x_send, x_recv, s_send, s_recv = scratch[1 + len(rounds) :]
    me = lax.axis_index("blk")
    partner = flipped(me, bits)
    peers = [[group_peer(me, stride, size, k) for k in range(1, size)] for stride, size in rounds]
    greeted = ([partner] if bits else []) + [peer for group in peers for peer in group]

    barrier = pltpu.get_barrier_semaphore()
    for device in greeted:
        pl.semaphore_signal(barrier, inc=1, device_id=(device,), device_id_type=MESH)
    pl.semaphore_wait(barrier, len(greeted))

    if bits:
        block = pltpu.make_async_remote_copy(
            src_ref=x_ref, dst_ref=y_ref, send_sem=x_send, recv_sem=x_recv,
            device_id=(partner,), device_id_type=MESH,
        )
    else:
        block = pltpu.make_async_copy(x_ref, y_ref, x_recv)
    block.start()

    if rounds:
        total = s_ref[...]
        for r, group in enumerate(peers):
            held[r] = total
            for k, peer in enumerate(group):
                pltpu.make_async_remote_copy(
                    src_ref=held.at[r], dst_ref=got[r].at[k], send_sem=s_send.at[r], recv_sem=s_recv.at[r],
                    device_id=(peer,), device_id_type=MESH,
                ).start()
            pltpu.make_async_copy(got[r], got[r], s_recv.at[r]).wait()
            total = total + jnp.sum(got[r][...], axis=0)
        t_ref[...] = total
        for r in range(len(rounds)):
            pltpu.make_async_copy(got[r], got[r], s_send.at[r]).wait()
    else:
        t_ref[...] = s_ref[...]
    block.wait()


def stage_call(bits, rounds, collective_id, x, s):
    anywhere = pl.BlockSpec(memory_space=pl.ANY)
    vmem = pl.BlockSpec(memory_space=pltpu.VMEM)
    return pl.pallas_call(
        functools.partial(stage_kernel, bits, rounds),
        out_shape=(jax.ShapeDtypeStruct(x.shape, x.dtype), jax.ShapeDtypeStruct(s.shape, s.dtype)),
        in_specs=[anywhere, vmem],
        out_specs=(anywhere, vmem),
        scratch_shapes=[
            pltpu.VMEM((max(1, len(rounds)),) + s.shape, F32),
            *[pltpu.VMEM((size - 1,) + s.shape, F32) for _, size in rounds],
            pltpu.SemaphoreType.DMA,
            pltpu.SemaphoreType.DMA,
            pltpu.SemaphoreType.DMA((max(1, len(rounds)),)),
            pltpu.SemaphoreType.DMA((max(1, len(rounds)),)),
        ],
        compiler_params=pltpu.CompilerParams(collective_id=collective_id, has_side_effects=True),
        name=f"exchange_{collective_id}",
    )(x, s)


def stage(mask, stage_bits, rounds, first_id, x, s):
    choice = sum(jnp.bitwise_and(jnp.right_shift(mask, bit), 1) << k for k, bit in enumerate(stage_bits))

    def branch(value):
        bits = tuple(bit for k, bit in enumerate(stage_bits) if value >> k & 1)
        return lambda x, s: stage_call(bits, rounds, first_id + value, x, s)

    return lax.switch(choice, [branch(value) for value in range(1 << len(stage_bits))], x, s)


def exchange(mask, x, s):
    x, s = stage(mask, STAGE_A, SUM_A, 0, x, s)
    x, s = stage(mask, STAGE_B, SUM_B, 16, x, s)
    flip = jnp.bitwise_and(jnp.right_shift(mask, CORE_BIT), 1)

    def cross(x, s):
        return stage_call((CORE_BIT,), (), 32, x, s)

    return lax.cond(flip == 1, cross, lambda x, s: (x, s), x, s)


def sub_epoch_kernel(
    sub, rows, cols, counts, mean_in, totals, users_in, ubias_in, packed_in, ratings, observed,
    users, ubias, packed, sums, mean_out,
    ubias_wide, items_t, ibias_wide, rating_buf, seen_buf, rating_sem, seen_sem,
):
    count = counts[sub]

    def fetch(t):
        return (
            pltpu.make_async_copy(ratings.at[sub, 0, t], rating_buf.at[t], rating_sem.at[t]),
            pltpu.make_async_copy(observed.at[sub, 0, t], seen_buf.at[t], seen_sem.at[t]),
        )

    def start(t, carry):
        for copy in fetch(t):
            copy.start()
        return carry

    lax.fori_loop(0, count, start, 0)

    mean = mean_in[...]
    if sub:
        total = jnp.sum(totals[...], axis=1, keepdims=True)
        mean = mean + mean_rate * total[0:1] / total[1:2]
    mean_out[...] = jnp.broadcast_to(mean, (1, TILE))
    mean = jnp.broadcast_to(mean, (8, TILE))

    diagonal = lax.broadcasted_iota(jnp.int32, (TILE, TILE), 0) == lax.broadcasted_iota(jnp.int32, (TILE, TILE), 1)
    for a in range(ROW_TILES):
        across = jnp.where(diagonal, ubias_in[a : a + 1, :], 0.0)
        ubias_wide[a * TILE : (a + 1) * TILE, :] = jnp.broadcast_to(
            jnp.sum(across, axis=1, keepdims=True), (TILE, TILE)
        )
        users[a * TILE : (a + 1) * TILE, :] = users_in[a * TILE : (a + 1) * TILE, :]
    for c in range(COL_TILES):
        items_t[c] = packed_in[c * TILE : (c + 1) * TILE, :].T
        ibias_wide[c] = jnp.broadcast_to(packed_in[ITEM_ROWS + c : ITEM_ROWS + c + 1, :], (8, TILE))

    learn_rate = step_scale / TILE

    def slot(t, carry):
        err_sum, obs_sum = carry
        row0 = pl.multiple_of(rows[sub, t] * TILE, TILE)
        c = cols[sub, t]
        for copy in fetch(t):
            copy.wait()
        u = users[pl.ds(row0, TILE), :]
        bu = ubias_wide[pl.ds(row0, TILE), :]
        vt = items_t[c]
        bv = ibias_wide[c]
        uh = u.astype(BF16)
        vht = vt.astype(BF16)
        obs = seen_buf[t].astype(F32)
        known = rating_buf[t].astype(F32) - bu
        known = (known.reshape(TILE // 8, 8, TILE) - (mean + bv)[None]).reshape(TILE, TILE)
        score = jnp.dot(uh, vht, preferred_element_type=F32)
        err = obs * (known - score)
        eh = err.astype(BF16)
        grad_u = lax.dot_general(eh, vht, (((1,), (1,)), ((), ())), preferred_element_type=F32)
        grad_vt = jnp.dot(uh.T, eh, preferred_element_type=F32)
        err_rows = jnp.sum(err, axis=1, keepdims=True)
        err_cols = jnp.sum(err.reshape(TILE // 8, 8, TILE), axis=0)
        users[pl.ds(row0, TILE), :] = u + learn_rate * (grad_u - shrink * u)
        items_t[c] = vt + learn_rate * (grad_vt - shrink * vt)
        ubias_wide[pl.ds(row0, TILE), :] = bu + bias_rate * (err_rows - shrink * bu)
        ibias_wide[c] = bv + bias_rate * (jnp.sum(err_cols, axis=0, keepdims=True) - shrink * bv)
        return err_sum + err_cols, obs_sum + jnp.sum(obs.reshape(TILE // 8, 8, TILE), axis=0)

    zero = jnp.zeros((8, TILE), F32)
    err_sum, obs_sum = lax.fori_loop(0, count, slot, (zero, zero))

    sums[0:1, :] = jnp.sum(err_sum, axis=0, keepdims=True)
    sums[1:2, :] = jnp.sum(obs_sum, axis=0, keepdims=True)
    sums[2:8, :] = jnp.zeros((6, TILE), F32)
    for a in range(ROW_TILES):
        wide = ubias_wide[a * TILE : (a + 1) * TILE, :]
        ubias[a : a + 1, :] = jnp.sum(jnp.where(diagonal, wide, 0.0), axis=0, keepdims=True)
    for c in range(COL_TILES):
        packed[c * TILE : (c + 1) * TILE, :] = items_t[c].T
        packed[ITEM_ROWS + c : ITEM_ROWS + c + 1, :] = ibias_wide[c][0:1, :]
    packed[ITEM_ROWS + COL_TILES : PACKED, :] = jnp.zeros((PACKED - ITEM_ROWS - COL_TILES, TILE), F32)


def sub_epoch(sub, rows, cols, counts, mean, totals, users, ubias, packed, ratings, observed):
    smem = pl.BlockSpec(memory_space=pltpu.SMEM)
    vmem = pl.BlockSpec(memory_space=pltpu.VMEM)
    anywhere = pl.BlockSpec(memory_space=pl.ANY)
    slots = ratings.shape[2]
    shape = lambda *dims: jax.ShapeDtypeStruct(dims, F32)
    return pl.pallas_call(
        functools.partial(sub_epoch_kernel, sub),
        out_shape=(shape(*users.shape), shape(*ubias.shape), shape(*packed.shape), shape(8, TILE), shape(1, TILE)),
        in_specs=[smem, smem, smem, vmem, vmem, vmem, vmem, vmem, anywhere, anywhere],
        out_specs=(vmem,) * 5,
        scratch_shapes=[
            pltpu.VMEM((ROW_TILES * TILE, TILE), F32),
            pltpu.VMEM((COL_TILES, TILE, TILE), F32),
            pltpu.VMEM((COL_TILES, 8, TILE), F32),
            pltpu.VMEM((slots, TILE, TILE), BF16),
            pltpu.VMEM((slots, TILE, TILE), jnp.int32),
            pltpu.SemaphoreType.DMA((slots,)),
            pltpu.SemaphoreType.DMA((slots,)),
        ],
        compiler_params=pltpu.CompilerParams(vmem_limit_bytes=24 << 20),
        name=f"sub_epoch_{sub}",
    )(rows, cols, counts, mean, totals, users, ubias, packed, ratings, observed)


def on_device(
    users,
    user_bias,
    items,
    item_bias,
    global_mean,
    item_owner,
    tile_rows,
    tile_cols,
    tile_counts,
    ratings,
    observed,
):
    masks = jnp.bitwise_xor(item_owner[:, 0], lax.axis_index("blk"))
    rows, cols, counts = tile_rows[:, 0], tile_cols[:, 0], tile_counts[:, 0]
    ubias = user_bias.reshape(ROW_TILES, TILE)
    pad = jnp.zeros((PACKED - ITEM_ROWS - COL_TILES, TILE), F32)
    packed = jnp.concatenate([items, item_bias.reshape(COL_TILES, TILE), pad], axis=0)
    mean = global_mean.reshape(1, 1)
    sums = jnp.zeros((8, TILE), F32)

    packed, totals = exchange(masks[0], packed, sums)
    users, ubias, packed, sums, mean = sub_epoch(
        0, rows, cols, counts, mean, totals, users, ubias, packed, ratings, observed
    )
    packed, totals = exchange(jnp.bitwise_xor(masks[0], masks[1]), packed, sums)
    users, ubias, packed, sums, mean = sub_epoch(
        1, rows, cols, counts, mean[:, :1], totals, users, ubias, packed, ratings, observed
    )
    packed, totals = exchange(masks[1], packed, sums)
    total = jnp.sum(totals, axis=1)
    mean = mean[0, 0] + mean_rate * total[0] / total[1]
    return (
        users,
        ubias.reshape(-1),
        packed[:ITEM_ROWS],
        packed[ITEM_ROWS : ITEM_ROWS + COL_TILES].reshape(-1),
        mean,
    )


def solution(mesh):
    in_specs = (
        P("blk", None),
        P("blk"),
        P("blk", None),
        P("blk"),
        P(),
        P(None, "blk"),
        P(None, "blk", None),
        P(None, "blk", None),
        P(None, "blk"),
        P(None, "blk", None, None, None),
        P(None, "blk", None, None, None),
    )
    out_specs = (P("blk", None), P("blk"), P("blk", None), P("blk"), P())
    return jax.shard_map(
        on_device, mesh=mesh, in_specs=in_specs, out_specs=out_specs, check_vma=False
    )
```

```python
import functools

import jax
import jax.numpy as jnp
from jax import lax
from jax.experimental import pallas as pl
from jax.experimental.pallas import tpu as pltpu
from jax.sharding import PartitionSpec as P

SUBEP = 2
TILE = 128
ROW_TILES = 8
COL_TILES = 4
ITEM_ROWS = COL_TILES * TILE
PACKED = ITEM_ROWS + 8

step_scale = 0.8
bias_rate = 0.005
shrink = 0.02
mean_rate = 0.5

F32 = jnp.float32
BF16 = jnp.bfloat16
MESH = pl.DeviceIdType.MESH

STAGE_A = (1, 2, 3, 7)
STAGE_B = (4, 5, 6, 8)
SUM_A = ((1, 2), (16, 8))
SUM_B = ((2, 8), (128, 4))
PIECES = ((0, 264), (264, 256))


def flipped(me, bits):
    other = me
    for bit in bits:
        taken = lax.rem(lax.div(me, 1 << bit), 2)
        other = other + (1 - 2 * taken) * (1 << bit)
    return other


def group_peer(me, stride, size, ahead):
    place = lax.rem(lax.div(me, stride), size)
    return me + (lax.rem(place + ahead, size) - place) * stride


def stage_kernel(bits, rounds, hand_on, x_ref, s_ref, y_ref, t_ref, *scratch):
    held, got = scratch[0], scratch[1 : 1 + len(rounds)]
    x_send, x_recv, s_send, s_recv, h_send, h_recv = scratch[1 + len(rounds) :]
    me = lax.axis_index("blk")
    partner = flipped(me, bits)
    sibling = flipped(me, (0,))
    peers = [[group_peer(me, stride, size, k) for k in range(1, size)] for stride, size in rounds]
    greeted = [peer for group in peers for peer in group]
    if bits:
        greeted = greeted + [partner]
    if hand_on:
        greeted = greeted + [sibling]

    barrier = pltpu.get_barrier_semaphore()
    for device in greeted:
        pl.semaphore_signal(barrier, inc=1, device_id=(device,), device_id_type=MESH)
    pl.semaphore_wait(barrier, len(greeted))

    def part(ref, piece):
        return ref.at[pl.ds(piece[0], piece[1])]

    here = y_ref.at[0] if hand_on else y_ref
    blocks = []
    for k, piece in enumerate(PIECES):
        if bits:
            block = pltpu.make_async_remote_copy(
                src_ref=part(x_ref, piece), dst_ref=part(here, piece), send_sem=x_send.at[k], recv_sem=x_recv.at[k],
                device_id=(partner,), device_id_type=MESH,
            )
        else:
            block = pltpu.make_async_copy(part(x_ref, piece), part(here, piece), x_recv.at[k])
        blocks.append(block)

    total = s_ref[...]
    for r, group in enumerate(peers):
        held[r] = total
        for k, peer in enumerate(group):
            pltpu.make_async_remote_copy(
                src_ref=held.at[r], dst_ref=got[r].at[k], send_sem=s_send.at[r], recv_sem=s_recv.at[r],
                device_id=(peer,), device_id_type=MESH,
            ).start()
        if r == 0:
            for block in blocks:
                block.start()
        pltpu.make_async_copy(got[r], got[r], s_recv.at[r]).wait()
        total = total + jnp.sum(got[r][...], axis=0)
    t_ref[...] = total
    for r in range(len(rounds)):
        pltpu.make_async_copy(got[r], got[r], s_send.at[r]).wait()

    handed = []
    for k, (piece, block) in enumerate(zip(PIECES, blocks)):
        if bits:
            block.wait_recv()
        else:
            block.wait()
        if hand_on:
            copy = pltpu.make_async_remote_copy(
                src_ref=part(here, piece), dst_ref=part(y_ref.at[1], piece), send_sem=h_send.at[k],
                recv_sem=h_recv.at[k], device_id=(sibling,), device_id_type=MESH,
            )
            copy.start()
            handed.append(copy)
    if bits:
        for block in blocks:
            block.wait_send()
    for copy in handed:
        copy.wait()


def stage_call(bits, rounds, hand_on, collective_id, x, s):
    anywhere = pl.BlockSpec(memory_space=pl.ANY)
    vmem = pl.BlockSpec(memory_space=pltpu.VMEM)
    out = ((2,) if hand_on else ()) + x.shape
    pieces = pltpu.SemaphoreType.DMA((len(PIECES),))
    turns = pltpu.SemaphoreType.DMA((len(rounds),))
    return pl.pallas_call(
        functools.partial(stage_kernel, bits, rounds, hand_on),
        out_shape=(jax.ShapeDtypeStruct(out, x.dtype), jax.ShapeDtypeStruct(s.shape, s.dtype)),
        in_specs=[anywhere, vmem],
        out_specs=(anywhere, vmem),
        scratch_shapes=[
            pltpu.VMEM((len(rounds),) + s.shape, F32),
            *[pltpu.VMEM((size - 1,) + s.shape, F32) for _, size in rounds],
            pieces,
            pieces,
            turns,
            turns,
            pieces,
            pieces,
        ],
        compiler_params=pltpu.CompilerParams(collective_id=collective_id, has_side_effects=True),
        name=f"exchange_{collective_id}",
    )(x, s)


def stage(mask, stage_bits, rounds, hand_on, first_id, x, s):
    choice = sum(jnp.bitwise_and(jnp.right_shift(mask, bit), 1) << k for k, bit in enumerate(stage_bits))

    def branch(value):
        bits = tuple(bit for k, bit in enumerate(stage_bits) if value >> k & 1)
        return lambda x, s: stage_call(bits, rounds, hand_on, first_id + value, x, s)

    return lax.switch(choice, [branch(value) for value in range(1 << len(stage_bits))], x, s)


def exchange(mask, x, s):
    x, s = stage(mask, STAGE_A, SUM_A, False, 0, x, s)
    x, s = stage(mask, STAGE_B, SUM_B, True, 16, x, s)
    return x, jnp.bitwise_and(mask, 1), s


def sub_epoch_kernel(
    sub, rows, cols, counts, place, mean_in, totals, users_in, ubias_in, pair, ratings, observed,
    users, ubias, packed, sums, mean_out,
    packed_in, packed_sem, users_sem, ubias_wide, items_t, ibias_wide, rating_buf, seen_buf, rating_sem, seen_sem,
):
    count = counts[sub]

    def fetch(t):
        return (
            pltpu.make_async_copy(ratings.at[sub, 0, t], rating_buf.at[t], rating_sem.at[t]),
            pltpu.make_async_copy(observed.at[sub, 0, t], seen_buf.at[t], seen_sem.at[t]),
        )

    def start(t, carry):
        for copy in fetch(t):
            copy.start()
        return carry

    arrival = pltpu.make_async_copy(pair.at[place[0]], packed_in, packed_sem)
    arrival.start()
    own = pltpu.make_async_copy(users_in, users, users_sem)
    own.start()
    lax.fori_loop(0, count, start, 0)

    mean = mean_in[...]
    if sub:
        total = jnp.sum(totals[...], axis=1, keepdims=True)
        mean = mean + mean_rate * total[0:1] / total[1:2]
    mean_out[...] = jnp.broadcast_to(mean, (1, TILE))
    mean = jnp.broadcast_to(mean, (8, TILE))

    diagonal = lax.broadcasted_iota(jnp.int32, (TILE, TILE), 0) == lax.broadcasted_iota(jnp.int32, (TILE, TILE), 1)
    for a in range(ROW_TILES):
        across = jnp.where(diagonal, ubias_in[a : a + 1, :], 0.0)
        ubias_wide[a * TILE : (a + 1) * TILE, :] = jnp.broadcast_to(
            jnp.sum(across, axis=1, keepdims=True), (TILE, TILE)
        )
    arrival.wait()
    for c in range(COL_TILES):
        items_t[c] = packed_in[c * TILE : (c + 1) * TILE, :].T
        ibias_wide[c] = jnp.broadcast_to(packed_in[ITEM_ROWS + c : ITEM_ROWS + c + 1, :], (8, TILE))

    own.wait()
    learn_rate = step_scale / TILE

    def slot(t, carry):
        err_sum, obs_sum = carry
        row0 = pl.multiple_of(rows[sub, t] * TILE, TILE)
        c = cols[sub, t]
        for copy in fetch(t):
            copy.wait()
        u = users[pl.ds(row0, TILE), :]
        bu = ubias_wide[pl.ds(row0, TILE), :]
        vt = items_t[c]
        bv = ibias_wide[c]
        uh = u.astype(BF16)
        vht = vt.astype(BF16)
        obs = seen_buf[t].astype(F32)
        known = rating_buf[t].astype(F32) - bu
        known = (known.reshape(TILE // 8, 8, TILE) - (mean + bv)[None]).reshape(TILE, TILE)
        score = jnp.dot(uh, vht, preferred_element_type=F32)
        err = obs * (known - score)
        eh = err.astype(BF16)
        grad_u = lax.dot_general(eh, vht, (((1,), (1,)), ((), ())), preferred_element_type=F32)
        grad_vt = jnp.dot(uh.T, eh, preferred_element_type=F32)
        err_rows = jnp.sum(err, axis=1, keepdims=True)
        err_cols = jnp.sum(err.reshape(TILE // 8, 8, TILE), axis=0)
        users[pl.ds(row0, TILE), :] = u + learn_rate * (grad_u - shrink * u)
        items_t[c] = vt + learn_rate * (grad_vt - shrink * vt)
        ubias_wide[pl.ds(row0, TILE), :] = bu + bias_rate * (err_rows - shrink * bu)
        ibias_wide[c] = bv + bias_rate * (jnp.sum(err_cols, axis=0, keepdims=True) - shrink * bv)
        return err_sum + err_cols, obs_sum + jnp.sum(obs.reshape(TILE // 8, 8, TILE), axis=0)

    zero = jnp.zeros((8, TILE), F32)
    err_sum, obs_sum = lax.fori_loop(0, count, slot, (zero, zero))

    sums[0:1, :] = jnp.sum(err_sum, axis=0, keepdims=True)
    sums[1:2, :] = jnp.sum(obs_sum, axis=0, keepdims=True)
    sums[2:8, :] = jnp.zeros((6, TILE), F32)
    for a in range(ROW_TILES):
        wide = ubias_wide[a * TILE : (a + 1) * TILE, :]
        ubias[a : a + 1, :] = jnp.sum(jnp.where(diagonal, wide, 0.0), axis=0, keepdims=True)
    for c in range(COL_TILES):
        packed[c * TILE : (c + 1) * TILE, :] = items_t[c].T
        packed[ITEM_ROWS + c : ITEM_ROWS + c + 1, :] = ibias_wide[c][0:1, :]
    packed[ITEM_ROWS + COL_TILES : PACKED, :] = jnp.zeros((PACKED - ITEM_ROWS - COL_TILES, TILE), F32)


def sub_epoch(sub, rows, cols, counts, place, mean, totals, users, ubias, pair, ratings, observed):
    smem = pl.BlockSpec(memory_space=pltpu.SMEM)
    vmem = pl.BlockSpec(memory_space=pltpu.VMEM)
    anywhere = pl.BlockSpec(memory_space=pl.ANY)
    slots = ratings.shape[2]
    shape = lambda *dims: jax.ShapeDtypeStruct(dims, F32)
    return pl.pallas_call(
        functools.partial(sub_epoch_kernel, sub),
        out_shape=(shape(*users.shape), shape(*ubias.shape), shape(*pair.shape[1:]), shape(8, TILE), shape(1, TILE)),
        in_specs=[smem, smem, smem, smem, vmem, vmem, anywhere, vmem, anywhere, anywhere, anywhere],
        out_specs=(vmem,) * 5,
        scratch_shapes=[
            pltpu.VMEM(pair.shape[1:], F32),
            pltpu.SemaphoreType.DMA,
            pltpu.SemaphoreType.DMA,
            pltpu.VMEM((ROW_TILES * TILE, TILE), F32),
            pltpu.VMEM((COL_TILES, TILE, TILE), F32),
            pltpu.VMEM((COL_TILES, 8, TILE), F32),
            pltpu.VMEM((slots, TILE, TILE), BF16),
            pltpu.VMEM((slots, TILE, TILE), jnp.int32),
            pltpu.SemaphoreType.DMA((slots,)),
            pltpu.SemaphoreType.DMA((slots,)),
        ],
        compiler_params=pltpu.CompilerParams(vmem_limit_bytes=24 << 20),
        name=f"sub_epoch_{sub}",
    )(rows, cols, counts, place.reshape(1), mean, totals, users, ubias, pair, ratings, observed)


def on_device(
    users,
    user_bias,
    items,
    item_bias,
    global_mean,
    item_owner,
    tile_rows,
    tile_cols,
    tile_counts,
    ratings,
    observed,
):
    masks = jnp.bitwise_xor(item_owner[:, 0], lax.axis_index("blk"))
    rows, cols, counts = tile_rows[:, 0], tile_cols[:, 0], tile_counts[:, 0]
    ubias = user_bias.reshape(ROW_TILES, TILE)
    pad = jnp.zeros((PACKED - ITEM_ROWS - COL_TILES, TILE), F32)
    packed = jnp.concatenate([items, item_bias.reshape(COL_TILES, TILE), pad], axis=0)
    mean = global_mean.reshape(1, 1)

    pair, place, totals = exchange(masks[0], packed, ubias)
    users, ubias, packed, sums, mean = sub_epoch(
        0, rows, cols, counts, place, mean, totals, users, ubias, pair, ratings, observed
    )
    pair, place, totals = exchange(jnp.bitwise_xor(masks[0], masks[1]), packed, sums)
    users, ubias, packed, sums, mean = sub_epoch(
        1, rows, cols, counts, place, mean[:, :1], totals, users, ubias, pair, ratings, observed
    )
    pair, place, totals = exchange(masks[1], packed, sums)
    packed = lax.dynamic_index_in_dim(pair, place, 0, keepdims=False)
    total = jnp.sum(totals, axis=1)
    mean = mean[0, 0] + mean_rate * total[0] / total[1]
    return (
        users,
        ubias.reshape(-1),
        packed[:ITEM_ROWS],
        packed[ITEM_ROWS : ITEM_ROWS + COL_TILES].reshape(-1),
        mean,
    )


def solution(mesh):
    in_specs = (
        P("blk", None),
        P("blk"),
        P("blk", None),
        P("blk"),
        P(),
        P(None, "blk"),
        P(None, "blk", None),
        P(None, "blk", None),
        P(None, "blk"),
        P(None, "blk", None, None, None),
        P(None, "blk", None, None, None),
    )
    out_specs = (P("blk", None), P("blk"), P("blk", None), P("blk"), P())
    return jax.shard_map(
        on_device, mesh=mesh, in_specs=in_specs, out_specs=out_specs, check_vma=False
    )
```

```python
import functools

import jax
import jax.numpy as jnp
from jax import lax
from jax.experimental import pallas as pl
from jax.experimental.pallas import tpu as pltpu
from jax.sharding import PartitionSpec as P

SUBEP = 2
TILE = 128
ROW_TILES = 8
COL_TILES = 4
ITEM_ROWS = COL_TILES * TILE
PACKED = ITEM_ROWS + 8

step_scale = 0.8
bias_rate = 0.005
shrink = 0.02
mean_rate = 0.5

F32 = jnp.float32
BF16 = jnp.bfloat16
MESH = pl.DeviceIdType.MESH

STAGE_A = (1, 2, 3, 7)
STAGE_B = (4, 5, 6, 8)
SUM_A = ((1, 2), (16, 8))
SUM_B = ((2, 8), (128, 4))
GROUP = 4
VMEM_BYTES = 60 << 20
PIECES = ((0, 264), (264, 256))


def flipped(me, bits):
    other = me
    for bit in bits:
        taken = lax.rem(lax.div(me, 1 << bit), 2)
        other = other + (1 - 2 * taken) * (1 << bit)
    return other


def group_peer(me, stride, size, ahead):
    place = lax.rem(lax.div(me, stride), size)
    return me + (lax.rem(place + ahead, size) - place) * stride


def far_first(size):
    return sorted(range(1, size), key=lambda ahead: -min(ahead, size - ahead))


def stage_kernel(bits, rounds, hand_on, x_ref, s_ref, y_ref, t_ref, *scratch):
    held, got = scratch[0], scratch[1 : 1 + len(rounds)]
    x_send, x_recv, s_send, s_recv, h_send, h_recv = scratch[1 + len(rounds) :]
    me = lax.axis_index("blk")
    partner = flipped(me, bits)
    sibling = flipped(me, (0,))
    peers = [[group_peer(me, stride, size, k) for k in far_first(size)] for stride, size in rounds]
    greeted = ([partner] if bits else []) + [peer for group in reversed(peers) for peer in group]
    if hand_on:
        greeted = greeted + [sibling]

    barrier = pltpu.get_barrier_semaphore()
    for device in greeted:
        pl.semaphore_signal(barrier, inc=1, device_id=(device,), device_id_type=MESH)
    pl.semaphore_wait(barrier, len(greeted))

    def part(ref, piece):
        return ref.at[pl.ds(piece[0], piece[1])]

    here = y_ref.at[0] if hand_on else y_ref
    blocks = []
    for k, piece in enumerate(PIECES):
        if bits:
            block = pltpu.make_async_remote_copy(
                src_ref=part(x_ref, piece), dst_ref=part(here, piece), send_sem=x_send.at[k], recv_sem=x_recv.at[k],
                device_id=(partner,), device_id_type=MESH,
            )
        else:
            block = pltpu.make_async_copy(part(x_ref, piece), part(here, piece), x_recv.at[k])
        blocks.append(block)

    total = s_ref[...]
    for r, group in enumerate(peers):
        held[r] = total
        for k, peer in enumerate(group):
            pltpu.make_async_remote_copy(
                src_ref=held.at[r], dst_ref=got[r].at[k], send_sem=s_send.at[r], recv_sem=s_recv.at[r],
                device_id=(peer,), device_id_type=MESH,
            ).start()
        if r == 0:
            for block in blocks:
                block.start()
        pltpu.make_async_copy(got[r], got[r], s_recv.at[r]).wait()
        total = total + jnp.sum(got[r][...], axis=0)
    t_ref[...] = total
    for r in range(len(rounds)):
        pltpu.make_async_copy(got[r], got[r], s_send.at[r]).wait()

    handed = []
    for k, (piece, block) in enumerate(zip(PIECES, blocks)):
        if bits:
            block.wait_recv()
        else:
            block.wait()
        if hand_on:
            copy = pltpu.make_async_remote_copy(
                src_ref=part(here, piece), dst_ref=part(y_ref.at[1], piece), send_sem=h_send.at[k],
                recv_sem=h_recv.at[k], device_id=(sibling,), device_id_type=MESH,
            )
            copy.start()
            handed.append(copy)
    if bits:
        for block in blocks:
            block.wait_send()
    for copy in handed:
        copy.wait()


def stage_call(bits, rounds, hand_on, collective_id, x, s):
    anywhere = pl.BlockSpec(memory_space=pl.ANY)
    vmem = pl.BlockSpec(memory_space=pltpu.VMEM)
    out = ((2,) if hand_on else ()) + x.shape
    pieces = pltpu.SemaphoreType.DMA((len(PIECES),))
    turns = pltpu.SemaphoreType.DMA((len(rounds),))
    return pl.pallas_call(
        functools.partial(stage_kernel, bits, rounds, hand_on),
        out_shape=(jax.ShapeDtypeStruct(out, x.dtype), jax.ShapeDtypeStruct(s.shape, s.dtype)),
        in_specs=[anywhere, vmem],
        out_specs=(anywhere, vmem),
        scratch_shapes=[
            pltpu.VMEM((len(rounds),) + s.shape, F32),
            *[pltpu.VMEM((size - 1,) + s.shape, F32) for _, size in rounds],
            pieces,
            pieces,
            turns,
            turns,
            pieces,
            pieces,
        ],
        compiler_params=pltpu.CompilerParams(collective_id=collective_id, has_side_effects=True),
        name=f"exchange_{collective_id}",
    )(x, s)


def stage(mask, stage_bits, rounds, hand_on, first_id, x, s):
    low, high = stage_bits[0], stage_bits[3]
    choice = jnp.bitwise_and(jnp.right_shift(mask, low), 7) + jnp.bitwise_and(jnp.right_shift(mask, high - 3), 8)

    def branch(value):
        bits = tuple(bit for k, bit in enumerate(stage_bits) if value >> k & 1)
        return lambda x, s: stage_call(bits, rounds, hand_on, first_id + value, x, s)

    return lax.switch(choice, [branch(value) for value in range(1 << len(stage_bits))], x, s)


def exchange(mask, x, s):
    x, s = stage(mask, STAGE_A, SUM_A, False, 0, x, s)
    x, s = stage(mask, STAGE_B, SUM_B, True, 16, x, s)
    return x, jnp.bitwise_and(mask, 1), s


def sub_epoch_kernel(
    sub, rows, cols, counts, place, mean_in, totals, users_in, ubias_in, pair, ratings, observed,
    users_out, ubias, packed, sums, mean_out,
    users, ubias_buf, users_sem, ubias_sem, ubias_wide, items_t, ibias_wide, rating_buf, seen_buf, rating_sem, seen_sem,
):
    count = counts[sub]

    def fetch(group):
        part = pl.ds(group * GROUP, GROUP)
        return (
            pltpu.make_async_copy(ratings.at[sub, 0, part], rating_buf.at[part], rating_sem.at[group]),
            pltpu.make_async_copy(observed.at[sub, 0, part], seen_buf.at[part], seen_sem.at[group]),
        )

    def fetched(group, carry):
        for copy in fetch(group):
            copy.wait()
        return carry

    groups = ratings.shape[2] // GROUP
    biases = pltpu.make_async_copy(ubias_in, ubias_buf, ubias_sem)
    biases.start()
    own = pltpu.make_async_copy(users_in, users, users_sem)
    own.start()
    for group in range(groups):
        for copy in fetch(group):
            copy.start()

    mean = mean_in[...]
    if sub:
        total = jnp.sum(totals[...], axis=1, keepdims=True)
        mean = mean + mean_rate * total[0:1] / total[1:2]
    mean_out[...] = jnp.broadcast_to(mean, (1, TILE))
    mean = jnp.broadcast_to(mean, (8, TILE))

    here = place[0]
    for c in range(COL_TILES):
        items_t[c] = pair[here, c * TILE : (c + 1) * TILE, :].T
    ibias_in = pair[here, ITEM_ROWS : ITEM_ROWS + 8, :]
    for c in range(COL_TILES):
        ibias_wide[c] = jnp.broadcast_to(ibias_in[c : c + 1, :], (8, TILE))
    diagonal = lax.broadcasted_iota(jnp.int32, (TILE, TILE), 0) == lax.broadcasted_iota(jnp.int32, (TILE, TILE), 1)
    biases.wait()
    for a in range(ROW_TILES):
        across = jnp.where(diagonal, ubias_buf[a : a + 1, :], 0.0)
        ubias_wide[a * TILE : (a + 1) * TILE, :] = jnp.broadcast_to(
            jnp.sum(across, axis=1, keepdims=True), (TILE, TILE)
        )
    own.wait()
    learn_rate = step_scale / TILE

    def slot(t, carry):
        err_sum, obs_sum = carry
        row0 = pl.multiple_of(rows[sub, t] * TILE, TILE)
        c = cols[sub, t]

        @pl.when(lax.rem(t, GROUP) == 0)
        def _():
            fetched(lax.div(t, GROUP), 0)

        u = users[pl.ds(row0, TILE), :]
        bu = ubias_wide[pl.ds(row0, TILE), :]
        vt = items_t[c]
        bv = ibias_wide[c]
        uh = u.astype(BF16)
        vht = vt.astype(BF16)
        obs = seen_buf[t].astype(F32)
        known = rating_buf[t].astype(F32) - bu
        known = (known.reshape(TILE // 8, 8, TILE) - (mean + bv)[None]).reshape(TILE, TILE)
        score = jnp.dot(uh, vht, preferred_element_type=F32)
        err = obs * (known - score)
        eh = err.astype(BF16)
        grad_u = lax.dot_general(eh, vht, (((1,), (1,)), ((), ())), preferred_element_type=F32)
        grad_vt = jnp.dot(uh.T, eh, preferred_element_type=F32)
        err_rows = jnp.sum(err, axis=1, keepdims=True)
        err_cols = jnp.sum(err.reshape(TILE // 8, 8, TILE), axis=0)
        users[pl.ds(row0, TILE), :] = u + learn_rate * (grad_u - shrink * u)
        items_t[c] = vt + learn_rate * (grad_vt - shrink * vt)
        ubias_wide[pl.ds(row0, TILE), :] = bu + bias_rate * (err_rows - shrink * bu)
        ibias_wide[c] = bv + bias_rate * (jnp.sum(err_cols, axis=0, keepdims=True) - shrink * bv)
        return err_sum + err_cols, obs_sum + jnp.sum(obs.reshape(TILE // 8, 8, TILE), axis=0)

    zero = jnp.zeros((8, TILE), F32)
    err_sum, obs_sum = lax.fori_loop(0, count, slot, (zero, zero))

    users_back = pltpu.make_async_copy(users, users_out, users_sem)
    users_back.start()

    for c in range(COL_TILES):
        packed[c * TILE : (c + 1) * TILE, :] = items_t[c].T
        packed[ITEM_ROWS + c : ITEM_ROWS + c + 1, :] = ibias_wide[c][0:1, :]
    packed[ITEM_ROWS + COL_TILES : PACKED, :] = jnp.zeros((PACKED - ITEM_ROWS - COL_TILES, TILE), F32)
    sums[0:1, :] = jnp.sum(err_sum, axis=0, keepdims=True)
    sums[1:2, :] = jnp.sum(obs_sum, axis=0, keepdims=True)
    sums[2:8, :] = jnp.zeros((6, TILE), F32)
    for a in range(ROW_TILES):
        wide = ubias_wide[a * TILE : (a + 1) * TILE, :]
        ubias[a : a + 1, :] = jnp.sum(jnp.where(diagonal, wide, 0.0), axis=0, keepdims=True)
    lax.fori_loop(lax.div(count + GROUP - 1, GROUP), groups, fetched, 0)
    users_back.wait()


def sub_epoch(sub, rows, cols, counts, place, mean, totals, users, ubias, pair, ratings, observed):
    smem = pl.BlockSpec(memory_space=pltpu.SMEM)
    vmem = pl.BlockSpec(memory_space=pltpu.VMEM)
    anywhere = pl.BlockSpec(memory_space=pl.ANY)
    slots = ratings.shape[2]
    shape = lambda *dims: jax.ShapeDtypeStruct(dims, F32)
    return pl.pallas_call(
        functools.partial(sub_epoch_kernel, sub),
        out_shape=(shape(*users.shape), shape(*ubias.shape), shape(*pair.shape[1:]), shape(8, TILE), shape(1, TILE)),
        in_specs=[smem, smem, smem, smem, vmem, vmem, anywhere, anywhere, vmem, anywhere, anywhere],
        out_specs=(anywhere, vmem, vmem, vmem, vmem),
        scratch_shapes=[
            pltpu.VMEM(users.shape, F32),
            pltpu.VMEM(ubias.shape, F32),
            pltpu.SemaphoreType.DMA,
            pltpu.SemaphoreType.DMA,
            pltpu.VMEM((ROW_TILES * TILE, TILE), F32),
            pltpu.VMEM((COL_TILES, TILE, TILE), F32),
            pltpu.VMEM((COL_TILES, 8, TILE), F32),
            pltpu.VMEM((slots, TILE, TILE), BF16),
            pltpu.VMEM((slots, TILE, TILE), jnp.int32),
            pltpu.SemaphoreType.DMA((slots // GROUP,)),
            pltpu.SemaphoreType.DMA((slots // GROUP,)),
        ],
        compiler_params=pltpu.CompilerParams(vmem_limit_bytes=VMEM_BYTES),
        name=f"sub_epoch_{sub}",
    )(rows, cols, counts, place.reshape(1), mean, totals, users, ubias, pair, ratings, observed)


def finish_kernel(place, mean_in, totals, pair, items_out, ibias_out, mean_out, items_sem):
    here = place[0]
    items = pltpu.make_async_copy(pair.at[here, pl.ds(0, ITEM_ROWS)], items_out, items_sem)
    items.start()
    ibias_out[...] = pair[here, ITEM_ROWS : ITEM_ROWS + 8, :][:COL_TILES]
    total = jnp.sum(totals[...], axis=1, keepdims=True)
    mean_out[...] = mean_in[:, 0:1] + mean_rate * total[0:1] / total[1:2]
    items.wait()


def finish(place, mean, totals, pair):
    smem = pl.BlockSpec(memory_space=pltpu.SMEM)
    vmem = pl.BlockSpec(memory_space=pltpu.VMEM)
    anywhere = pl.BlockSpec(memory_space=pl.ANY)
    shape = lambda *dims: jax.ShapeDtypeStruct(dims, F32)
    return pl.pallas_call(
        finish_kernel,
        out_shape=(shape(ITEM_ROWS, TILE), shape(COL_TILES, TILE), shape(1, 1)),
        in_specs=[smem, vmem, vmem, vmem],
        out_specs=(anywhere, vmem, vmem),
        scratch_shapes=[pltpu.SemaphoreType.DMA],
        name="finish",
    )(place.reshape(1), mean, totals, pair)


def on_device(
    users,
    user_bias,
    items,
    item_bias,
    global_mean,
    item_owner,
    tile_rows,
    tile_cols,
    tile_counts,
    ratings,
    observed,
):
    me = lax.axis_index("blk")
    masks = [jnp.bitwise_xor(item_owner[sub, 0], me) for sub in range(SUBEP)]
    rows, cols, counts = tile_rows[:, 0], tile_cols[:, 0], tile_counts[:, 0]
    ubias = user_bias.reshape(ROW_TILES, TILE)
    pad = jnp.zeros((PACKED - ITEM_ROWS - COL_TILES, TILE), F32)
    packed = jnp.concatenate([items, item_bias.reshape(COL_TILES, TILE), pad], axis=0)
    mean = global_mean.reshape(1, 1)

    pair, place, totals = exchange(masks[0], packed, ubias)
    users, ubias, packed, sums, mean = sub_epoch(
        0, rows, cols, counts, place, mean, totals, users, ubias, pair, ratings, observed
    )
    pair, place, totals = exchange(jnp.bitwise_xor(masks[0], masks[1]), packed, sums)
    users, ubias, packed, sums, mean = sub_epoch(
        1, rows, cols, counts, place, mean[:, :1], totals, users, ubias, pair, ratings, observed
    )
    pair, place, totals = exchange(masks[1], packed, sums)
    items, item_bias, mean = finish(place, mean, totals, pair)
    return (users, ubias.reshape(-1), items, item_bias.reshape(-1), mean.reshape(()))


def solution(mesh):
    in_specs = (
        P("blk", None),
        P("blk"),
        P("blk", None),
        P("blk"),
        P(),
        P(None, "blk"),
        P(None, "blk", None),
        P(None, "blk", None),
        P(None, "blk"),
        P(None, "blk", None, None, None),
        P(None, "blk", None, None, None),
    )
    out_specs = (P("blk", None), P("blk"), P("blk", None), P("blk"), P())
    return jax.shard_map(
        on_device, mesh=mesh, in_specs=in_specs, out_specs=out_specs, check_vma=False
    )
```

```python
import functools

import jax
import jax.numpy as jnp
from jax import lax
from jax.experimental import pallas as pl
from jax.experimental.pallas import tpu as pltpu
from jax.sharding import PartitionSpec as P

SUBEP = 2
TILE = 128
ROW_TILES = 8
COL_TILES = 4
ITEM_ROWS = COL_TILES * TILE

step_scale = 0.8
bias_rate = 0.005
shrink = 0.02
mean_rate = 0.5

F32 = jnp.float32
BF16 = jnp.bfloat16
MESH = pl.DeviceIdType.MESH

STAGE_A = (1, 2, 3, 7)
STAGE_B = (4, 5, 6, 8)
SUM_A = ((1, 2), (16, 8))
SUM_B = ((2, 8), (128, 4))
GROUP = 4
VMEM_BYTES = 60 << 20


def flipped(me, bits):
    other = me
    for bit in bits:
        taken = lax.rem(lax.div(me, 1 << bit), 2)
        other = other + (1 - 2 * taken) * (1 << bit)
    return other


def group_peer(me, stride, size, ahead):
    place = lax.rem(lax.div(me, stride), size)
    return me + (lax.rem(place + ahead, size) - place) * stride


def far_first(size):
    return sorted(range(1, size), key=lambda ahead: -min(ahead, size - ahead))


def stage_kernel(bits, rounds, hand_on, items, ibias, sums, items_out, ibias_out, totals, *scratch):
    held, got = scratch[0], scratch[1 : 1 + len(rounds)]
    b_send, b_recv, s_send, s_recv, h_send, h_recv = scratch[1 + len(rounds) :]
    me = lax.axis_index("blk")
    partner = flipped(me, bits)
    sibling = flipped(me, (0,))
    peers = [[group_peer(me, stride, size, k) for k in far_first(size)] for stride, size in rounds]
    greeted = ([partner] if bits else []) + [peer for group in reversed(peers) for peer in group]
    if hand_on:
        greeted = greeted + [sibling]

    barrier = pltpu.get_barrier_semaphore()
    for device in greeted:
        pl.semaphore_signal(barrier, inc=1, device_id=(device,), device_id_type=MESH)
    pl.semaphore_wait(barrier, len(greeted))

    blocks = []
    for k, (source, target) in enumerate(((items, items_out), (ibias, ibias_out))):
        here = target.at[0] if hand_on else target
        if bits:
            block = pltpu.make_async_remote_copy(
                src_ref=source, dst_ref=here, send_sem=b_send.at[k], recv_sem=b_recv.at[k],
                device_id=(partner,), device_id_type=MESH,
            )
        else:
            block = pltpu.make_async_copy(source, here, b_recv.at[k])
        blocks.append(block)

    total = sums[...]
    handed = []
    for r, group in enumerate(peers):
        held[r] = total
        for k, peer in enumerate(group):
            pltpu.make_async_remote_copy(
                src_ref=held.at[r], dst_ref=got[r].at[k], send_sem=s_send.at[r], recv_sem=s_recv.at[r],
                device_id=(peer,), device_id_type=MESH,
            ).start()
        if r == 0:
            for block in blocks:
                block.start()
        if r == len(peers) - 1:
            for k, (block, target) in enumerate(zip(blocks, (items_out, ibias_out))):
                if bits:
                    block.wait_recv()
                else:
                    block.wait()
                if hand_on:
                    copy = pltpu.make_async_remote_copy(
                        src_ref=target.at[0], dst_ref=target.at[1], send_sem=h_send.at[k], recv_sem=h_recv.at[k],
                        device_id=(sibling,), device_id_type=MESH,
                    )
                    copy.start()
                    handed.append(copy)
        pltpu.make_async_copy(got[r], got[r], s_recv.at[r]).wait()
        total = total + jnp.sum(got[r][...], axis=0)
    totals[...] = total
    for r in range(len(rounds)):
        pltpu.make_async_copy(got[r], got[r], s_send.at[r]).wait()
    if bits:
        for block in blocks:
            block.wait_send()
    for copy in handed:
        copy.wait()


def stage_call(bits, rounds, hand_on, collective_id, items, ibias, sums):
    anywhere = pl.BlockSpec(memory_space=pl.ANY)
    vmem = pl.BlockSpec(memory_space=pltpu.VMEM)
    slots = (2,) if hand_on else ()
    two = pltpu.SemaphoreType.DMA((2,))
    turns = pltpu.SemaphoreType.DMA((len(rounds),))
    return pl.pallas_call(
        functools.partial(stage_kernel, bits, rounds, hand_on),
        out_shape=(
            jax.ShapeDtypeStruct(slots + items.shape, F32),
            jax.ShapeDtypeStruct(slots + ibias.shape, F32),
            jax.ShapeDtypeStruct(sums.shape, F32),
        ),
        in_specs=[anywhere, anywhere, vmem],
        out_specs=(anywhere, anywhere, vmem),
        scratch_shapes=[
            pltpu.VMEM((len(rounds),) + sums.shape, F32),
            *[pltpu.VMEM((size - 1,) + sums.shape, F32) for _, size in rounds],
            two,
            two,
            turns,
            turns,
            two,
            two,
        ],
        compiler_params=pltpu.CompilerParams(collective_id=collective_id, has_side_effects=True),
        name=f"exchange_{collective_id}",
    )(items, ibias, sums)


def stage(mask, stage_bits, rounds, hand_on, first_id, *block):
    low, high = stage_bits[0], stage_bits[3]
    choice = jnp.bitwise_and(jnp.right_shift(mask, low), 7) + jnp.bitwise_and(jnp.right_shift(mask, high - 3), 8)

    def branch(value):
        bits = tuple(bit for k, bit in enumerate(stage_bits) if value >> k & 1)
        return lambda *block: stage_call(bits, rounds, hand_on, first_id + value, *block)

    return lax.switch(choice, [branch(value) for value in range(1 << len(stage_bits))], *block)


def exchange(mask, items, ibias, sums):
    block = stage(mask, STAGE_A, SUM_A, False, 0, items, ibias, sums)
    items, ibias, totals = stage(mask, STAGE_B, SUM_B, True, 16, *block)
    return jnp.bitwise_and(mask, 1), totals, items, ibias


def sub_epoch_kernel(
    sub, rows, cols, counts, place, mean_in, totals, users_in, ubias_in, items_in, ibias_in, ratings, observed,
    users_out, ubias, items, ibias, sums, mean_out,
    users, ubias_buf, users_sem, ubias_sem, ubias_wide, items_t, ibias_wide, rating_buf, seen_buf, rating_sem, seen_sem,
):
    count = counts[sub]

    def fetch(group):
        part = pl.ds(group * GROUP, GROUP)
        return (
            pltpu.make_async_copy(ratings.at[sub, 0, part], rating_buf.at[part], rating_sem.at[group]),
            pltpu.make_async_copy(observed.at[sub, 0, part], seen_buf.at[part], seen_sem.at[group]),
        )

    def fetched(group, carry):
        for copy in fetch(group):
            copy.wait()
        return carry

    groups = ratings.shape[2] // GROUP
    biases = pltpu.make_async_copy(ubias_in, ubias_buf, ubias_sem)
    biases.start()
    own = pltpu.make_async_copy(users_in, users, users_sem)
    own.start()
    for group in range(groups):
        for copy in fetch(group):
            copy.start()

    mean = mean_in[...]
    if sub:
        total = jnp.sum(totals[...], axis=1, keepdims=True)
        mean = mean + mean_rate * total[0:1] / total[1:2]
    mean_out[...] = jnp.broadcast_to(mean, (1, TILE))
    mean = jnp.broadcast_to(mean, (8, TILE))

    here = place[0]
    for c in range(COL_TILES):
        items_t[c] = items_in[here, c * TILE : (c + 1) * TILE, :].T
        ibias_wide[c] = jnp.broadcast_to(ibias_in[here, c : c + 1, :], (8, TILE))
    diagonal = lax.broadcasted_iota(jnp.int32, (TILE, TILE), 0) == lax.broadcasted_iota(jnp.int32, (TILE, TILE), 1)
    biases.wait()
    for a in range(ROW_TILES):
        across = jnp.where(diagonal, ubias_buf[a : a + 1, :], 0.0)
        ubias_wide[a * TILE : (a + 1) * TILE, :] = jnp.broadcast_to(
            jnp.sum(across, axis=1, keepdims=True), (TILE, TILE)
        )
    own.wait()
    learn_rate = step_scale / TILE

    def slot(t, carry):
        err_sum, obs_sum = carry
        row0 = pl.multiple_of(rows[sub, t] * TILE, TILE)
        c = cols[sub, t]

        @pl.when(lax.rem(t, GROUP) == 0)
        def _():
            fetched(lax.div(t, GROUP), 0)

        u = users[pl.ds(row0, TILE), :]
        bu = ubias_wide[pl.ds(row0, TILE), :]
        vt = items_t[c]
        bv = ibias_wide[c]
        uh = u.astype(BF16)
        vht = vt.astype(BF16)
        obs = seen_buf[t].astype(F32)
        known = rating_buf[t].astype(F32) - bu
        known = (known.reshape(TILE // 8, 8, TILE) - (mean + bv)[None]).reshape(TILE, TILE)
        score = jnp.dot(uh, vht, preferred_element_type=F32)
        err = obs * (known - score)
        eh = err.astype(BF16)
        grad_u = lax.dot_general(eh, vht, (((1,), (1,)), ((), ())), preferred_element_type=F32)
        grad_vt = jnp.dot(uh.T, eh, preferred_element_type=F32)
        err_rows = jnp.sum(err, axis=1, keepdims=True)
        err_cols = jnp.sum(err.reshape(TILE // 8, 8, TILE), axis=0)
        users[pl.ds(row0, TILE), :] = u + learn_rate * (grad_u - shrink * u)
        items_t[c] = vt + learn_rate * (grad_vt - shrink * vt)
        ubias_wide[pl.ds(row0, TILE), :] = bu + bias_rate * (err_rows - shrink * bu)
        ibias_wide[c] = bv + bias_rate * (jnp.sum(err_cols, axis=0, keepdims=True) - shrink * bv)
        return err_sum + err_cols, obs_sum + jnp.sum(obs.reshape(TILE // 8, 8, TILE), axis=0)

    zero = jnp.zeros((8, TILE), F32)
    err_sum, obs_sum = lax.fori_loop(0, count, slot, (zero, zero))

    users_back = pltpu.make_async_copy(users, users_out, users_sem)
    users_back.start()

    for c in range(COL_TILES):
        items[c * TILE : (c + 1) * TILE, :] = items_t[c].T
        ibias[c : c + 1, :] = ibias_wide[c][0:1, :]
    sums[0:1, :] = jnp.sum(err_sum, axis=0, keepdims=True)
    sums[1:2, :] = jnp.sum(obs_sum, axis=0, keepdims=True)
    sums[2:8, :] = jnp.zeros((6, TILE), F32)
    for a in range(ROW_TILES):
        wide = ubias_wide[a * TILE : (a + 1) * TILE, :]
        ubias[a : a + 1, :] = jnp.sum(jnp.where(diagonal, wide, 0.0), axis=0, keepdims=True)
    lax.fori_loop(lax.div(count + GROUP - 1, GROUP), groups, fetched, 0)
    users_back.wait()


def sub_epoch(sub, rows, cols, counts, mean, users, ubias, place, totals, items, ibias, ratings, observed):
    smem = pl.BlockSpec(memory_space=pltpu.SMEM)
    vmem = pl.BlockSpec(memory_space=pltpu.VMEM)
    anywhere = pl.BlockSpec(memory_space=pl.ANY)
    slots = ratings.shape[2]
    shape = lambda *dims: jax.ShapeDtypeStruct(dims, F32)
    return pl.pallas_call(
        functools.partial(sub_epoch_kernel, sub),
        out_shape=(
            shape(*users.shape), shape(*ubias.shape), shape(*items.shape[1:]), shape(*ibias.shape[1:]),
            shape(8, TILE), shape(1, TILE),
        ),
        in_specs=[smem, smem, smem, smem, vmem, vmem, anywhere, anywhere, vmem, vmem, anywhere, anywhere],
        out_specs=(anywhere, vmem, vmem, vmem, vmem, vmem),
        scratch_shapes=[
            pltpu.VMEM(users.shape, F32),
            pltpu.VMEM(ubias.shape, F32),
            pltpu.SemaphoreType.DMA,
            pltpu.SemaphoreType.DMA,
            pltpu.VMEM((ROW_TILES * TILE, TILE), F32),
            pltpu.VMEM((COL_TILES, TILE, TILE), F32),
            pltpu.VMEM((COL_TILES, 8, TILE), F32),
            pltpu.VMEM((slots, TILE, TILE), BF16),
            pltpu.VMEM((slots, TILE, TILE), jnp.int32),
            pltpu.SemaphoreType.DMA((slots // GROUP,)),
            pltpu.SemaphoreType.DMA((slots // GROUP,)),
        ],
        compiler_params=pltpu.CompilerParams(vmem_limit_bytes=VMEM_BYTES),
        name=f"sub_epoch_{sub}",
    )(rows, cols, counts, place.reshape(1), mean, totals, users, ubias, items, ibias, ratings, observed)


def finish_kernel(place, mean_in, totals, items_in, ibias_in, items, ibias, mean_out, items_sem):
    here = place[0]
    copy = pltpu.make_async_copy(items_in.at[here], items, items_sem)
    copy.start()
    ibias[...] = ibias_in[here]
    total = jnp.sum(totals[...], axis=1, keepdims=True)
    mean_out[...] = mean_in[:, 0:1] + mean_rate * total[0:1] / total[1:2]
    copy.wait()


def finish(mean, place, totals, items, ibias):
    smem = pl.BlockSpec(memory_space=pltpu.SMEM)
    vmem = pl.BlockSpec(memory_space=pltpu.VMEM)
    anywhere = pl.BlockSpec(memory_space=pl.ANY)
    shape = lambda *dims: jax.ShapeDtypeStruct(dims, F32)
    return pl.pallas_call(
        finish_kernel,
        out_shape=(shape(*items.shape[1:]), shape(*ibias.shape[1:]), shape(1, 1)),
        in_specs=[smem, vmem, vmem, vmem, vmem],
        out_specs=(anywhere, vmem, vmem),
        scratch_shapes=[pltpu.SemaphoreType.DMA],
        name="finish",
    )(place.reshape(1), mean, totals, items, ibias)


def on_device(
    users,
    user_bias,
    items,
    item_bias,
    global_mean,
    item_owner,
    tile_rows,
    tile_cols,
    tile_counts,
    ratings,
    observed,
):
    me = lax.axis_index("blk")
    masks = [jnp.bitwise_xor(item_owner[sub, 0], me) for sub in range(SUBEP)]
    rows, cols, counts = tile_rows[:, 0], tile_cols[:, 0], tile_counts[:, 0]
    ubias = user_bias.reshape(ROW_TILES, TILE)
    ibias = item_bias.reshape(COL_TILES, TILE)
    mean = global_mean.reshape(1, 1)

    arrived = exchange(masks[0], items, ibias, ubias)
    users, ubias, items, ibias, sums, mean = sub_epoch(
        0, rows, cols, counts, mean, users, ubias, *arrived, ratings, observed
    )
    arrived = exchange(jnp.bitwise_xor(masks[0], masks[1]), items, ibias, sums)
    users, ubias, items, ibias, sums, mean = sub_epoch(
        1, rows, cols, counts, mean[:, :1], users, ubias, *arrived, ratings, observed
    )
    arrived = exchange(masks[1], items, ibias, sums)
    items, ibias, mean = finish(mean, *arrived)
    return (users, ubias.reshape(-1), items, ibias.reshape(-1), mean.reshape(()))


def solution(mesh):
    in_specs = (
        P("blk", None),
        P("blk"),
        P("blk", None),
        P("blk"),
        P(),
        P(None, "blk"),
        P(None, "blk", None),
        P(None, "blk", None),
        P(None, "blk"),
        P(None, "blk", None, None, None),
        P(None, "blk", None, None, None),
    )
    out_specs = (P("blk", None), P("blk"), P("blk", None), P("blk"), P())
    return jax.shard_map(
        on_device, mesh=mesh, in_specs=in_specs, out_specs=out_specs, check_vma=False
    )
```
